512 devices in a mesh: row: 16 (over y, x_hi), col: 32 (over x_lo, z, core).
Axes of the slice: x: 4 (x_hi: 2, x_lo: 2; x = x_hi * 2 + x_lo), y: 8, z: 8, core: 2. Of those that a mesh axis runs over, the one named last changes fastest.
Arguments:
- tokens: bfloat16 [2048, 4096], P('row', 'col'), may hold values from -6 to 6
- mixer_out: bfloat16 [2048, 8192], P('row', 'col'), may hold values from -6 to 6
- gate_weight: bfloat16 [4096, 8192], P('row', 'col'), may hold values from -0.09375 to 0.09375
- out_weight: bfloat16 [8192, 4096], P('row', 'col'), may hold values from -0.125 to 0.125
- out_grad: bfloat16 [2048, 4096], P('row', 'col'), may hold values from -6 to 6
Outputs:
- layer_out: bfloat16 [2048, 4096], P('row', 'col')
- mixer_grad: bfloat16 [2048, 8192], P('row', 'col')
- gate_weight_grad: bfloat16 [4096, 8192], P('row', 'col')
- out_weight_grad: bfloat16 [8192, 4096], P('row', 'col')
The draws below stay inside these ranges and needn't reach their ends.
All inputs are finite; a program needn't handle non-finite values.
Results may differ from the reference program's by a relative error of at most 0.0049.
Values may be sent and summed in bfloat16 or wider, within the bound.
No kernel may reach another device: no remote copies, remote signals or barrier semaphores. Data moves between devices by JAX's collectives and lax.ppermute only.
A program may use at most 64 MiB of HBM per device.

```python
import jax
import jax.numpy as jnp
from jax import lax

D = 4096
INNER = 8192
TOKENS = 2048


def with_spikes(values, stream_key, source, target, parts, factor):
    owner, partner = [(jnp.arange(values.shape[dim]) // (values.shape[dim] // parts)).reshape([-1 if axis == dim else 1 for axis in range(values.ndim)]) for dim in (source, target)]
    chosen = jax.random.permutation(stream_key, parts)[partner]
    strong = (owner == chosen) | (owner == (partner + parts // 2) % parts)
    return jnp.where(strong, factor * values, values)


def level_of(own_key, dims, pieces, low, top_value):
    gain, own = 1.0, jax.random.fold_in(own_key, 6)
    for dim, shards_of in pieces:
        heights = jnp.exp(jax.random.uniform(jax.random.fold_in(own, dim), (shards_of,), jnp.float32, low / len(pieces), top_value / len(pieces)))
        gain = gain * jnp.repeat(heights, dims[dim] // shards_of).reshape([-1 if axis == dim else 1 for axis in range(len(dims))])
    return gain


def normal_values(stream_key, shape, scale, limit, cuts=(), dtype=jnp.bfloat16):
    values = scale * jax.random.normal(stream_key, shape, jnp.float32)
    if cuts:
        values = values * level_of(stream_key, shape, cuts, -0.22, 0.18)
    return jnp.clip(values, -limit, limit).astype(dtype)


def noise_with(own_key, shape, width, most, pieces, heavy, kind=jnp.bfloat16):
    entries = width * jax.random.normal(own_key, shape, jnp.float32)
    if pieces:
        entries = entries * level_of(own_key, shape, pieces, -0.22, 0.18)
    return jnp.clip(with_spikes(entries, jax.random.fold_in(own_key, 3), *heavy), -most, most).astype(kind)


def setup_inputs(seed: int = 0) -> dict:
    streams_of = jax.random.split(jax.random.key(seed), 6)
    tokens = normal_values(streams_of[0], (TOKENS, D), 1.0, 6.0, ((0, 16), (1, 32)))
    mixer_out = normal_values(streams_of[1], (TOKENS, INNER), 1.0, 6.0, ((0, 16), (1, 32)))
    gate_weight = normal_values(streams_of[2], (D, INNER), D ** -0.5, 0.09375, ((0, 16), (1, 32)))
    out_weight = noise_with(streams_of[3], (INNER, D), INNER ** -0.5, 0.125, ((0, 16), (1, 32)), (1, 0, 32, 2.75))
    out_grad = normal_values(streams_of[4], (TOKENS, D), 1.0, 6.0, ((0, 16), (1, 32)))
    return dict(tokens=tokens, mixer_out=mixer_out, gate_weight=gate_weight, out_weight=out_weight, out_grad=out_grad)


def reference(tokens, mixer_out, gate_weight, out_weight, out_grad):
    gate_pre = jnp.dot(tokens, gate_weight, preferred_element_type=jnp.float32)
    gate_sig = jax.nn.sigmoid(gate_pre)
    gate_silu = gate_pre * gate_sig
    mixer_vals = mixer_out.astype(jnp.float32)
    gated = (mixer_vals * gate_silu).astype(jnp.bfloat16)
    layer_out = jnp.dot(gated, out_weight, preferred_element_type=jnp.float32).astype(jnp.bfloat16)
    hidden_grad = lax.dot_general(out_grad, out_weight, (((1,), (1,)), ((), ())), preferred_element_type=jnp.float32)
    mixer_grad = (hidden_grad * gate_silu).astype(jnp.bfloat16)
    pre_grad = (hidden_grad * mixer_vals * gate_sig * (1.0 + gate_pre * (1.0 - gate_sig))).astype(jnp.bfloat16)
    out_weight_grad = lax.dot_general(gated, out_grad, (((0,), (0,)), ((), ())), preferred_element_type=jnp.float32).astype(jnp.bfloat16)
    gate_weight_grad = lax.dot_general(tokens, pre_grad, (((0,), (0,)), ((), ())), preferred_element_type=jnp.float32).astype(jnp.bfloat16)
    return layer_out, mixer_grad, gate_weight_grad, out_weight_grad
```

```python
import jax
import jax.numpy as jnp
from jax import lax
from jax.sharding import Mesh, PartitionSpec as P

ROWS, COLS = ("y", "xh"), ("xl", "z", "c")
ALL = ROWS + COLS
N = 16


def device(r, j, core):
    return (r * N + j) * 2 + core


ALONG_J = [[[device(r, j, core) for j in range(N)] for r in range(N)] for core in (0, 1)]
ALONG_R = [[[device(r, j, core) for r in range(N)] for j in range(N)] for core in (0, 1)]
GROUPS_A = ALONG_J[0] + ALONG_R[1]
GROUPS_B = ALONG_R[0] + ALONG_J[1]
CHIPS = [(r, j) for r in range(N) for j in range(N)]
SWAP = [(d, d ^ 1) for d in range(2 * N * N)]
TURN_OWN = [p for r, j in CHIPS for p in ((device(r, j, 0), device(j, r, 0)), (device(r, j, 1), device(r, j, 1)))]
TURN_OTHER = [p for r, j in CHIPS for p in ((device(r, j, 1), device(j, r, 0)), (device(r, j, 0), device(r, j, 1)))]
CROSS = [p for r, j in CHIPS for p in ((device(r, j, 0), device(j, r, 1)), (device(r, j, 1), device(j, r, 0)))]


def trade(blocks, groups):
    return lax.all_to_all(blocks, ALL, split_axis=0, concat_axis=0, axis_index_groups=groups, tiled=True)


def gather(block, groups):
    out = trade(jnp.broadcast_to(block, (N,) + block.shape), groups)
    return out.reshape(N * block.shape[0], block.shape[1])


def reduce(partial, groups):
    blocks = partial.astype(jnp.bfloat16).reshape(N, partial.shape[0] // N, partial.shape[1])
    return jnp.sum(trade(blocks, groups).astype(jnp.float32), axis=0)


def fold(wide):
    half = wide.shape[1] // 2
    return jnp.concatenate([wide[:, :half], wide[:, half:]], axis=0)


def unfold(tall):
    half = tall.shape[0] // 2
    return jnp.concatenate([tall[:half], tall[half:]], axis=1)


def local(tokens, mixer_out, gate_weight, out_weight, out_grad):
    f32, bf16 = jnp.float32, jnp.bfloat16
    first = lax.axis_index("c") == 0
    own = lax.ppermute(jnp.where(first, tokens, out_grad), ALL, TURN_OWN)
    other = lax.ppermute(jnp.where(first, out_grad, tokens), ALL, TURN_OTHER)
    acts = jnp.concatenate([own, other], axis=1)
    out_t = out_weight.T
    weight_in = lax.ppermute(jnp.where(first, fold(out_t), gate_weight), ALL, SWAP)
    weight = jnp.where(
        first,
        jnp.concatenate([gate_weight, weight_in], axis=1),
        jnp.concatenate([out_t, unfold(weight_in)], axis=0),
    )
    mixer_in = lax.ppermute(mixer_out, ALL, SWAP)
    mixer_vals = jnp.concatenate([mixer_out, mixer_in], axis=1).astype(f32)

    acts_all = gather(acts, GROUPS_A)
    total = reduce(jnp.dot(acts_all, weight, preferred_element_type=f32), GROUPS_B)

    gate_pre = total
    gate_sig = jax.nn.sigmoid(gate_pre)
    gate_silu = gate_pre * gate_sig
    gated = (mixer_vals * gate_silu).astype(bf16)
    crossed = lax.ppermute(jnp.where(first, gated.astype(f32), total), ALL, CROSS)
    hidden_grad = crossed
    mixer_grad = (hidden_grad * gate_silu).astype(bf16)
    pre_grad = (hidden_grad * mixer_vals * gate_sig * (1.0 + gate_pre * (1.0 - gate_sig))).astype(bf16)
    units_all = gather(jnp.where(first, pre_grad, crossed.astype(bf16)), GROUPS_B)

    layer_pair = reduce(
        lax.dot_general(units_all, weight, (((1,), (1,)), ((), ())), preferred_element_type=f32), GROUPS_A
    ).astype(bf16)
    grads = lax.dot_general(
        acts_all, units_all, (((0,), (0,)), ((), ())), preferred_element_type=f32
    ).astype(bf16)

    inner, width = gate_weight.shape[1], out_grad.shape[1]
    mixer_grad_in = lax.ppermute(mixer_grad[:, inner:], ALL, SWAP)
    grads_in = lax.ppermute(jnp.where(first, grads[:, inner:], fold(grads[width:])), ALL, SWAP)
    layer_in = lax.ppermute(layer_pair[:, width:], ALL, SWAP)
    return (
        jnp.where(first, layer_in, layer_pair[:, :width]),
        jnp.where(first, mixer_grad[:, :inner], mixer_grad_in),
        jnp.where(first, grads[:, :inner], grads_in),
        jnp.where(first, unfold(grads_in), grads[:width]).T,
    )


def solution(mesh):
    fine = Mesh(mesh.devices.reshape(8, 2, 2, 8, 2), ALL)
    spec = P(ROWS, COLS)
    return jax.shard_map(local, mesh=fine, in_specs=(spec,) * 5, out_specs=(spec,) * 4, check_vma=False)
```

```python
import jax
import jax.numpy as jnp
from jax import lax
from jax.sharding import Mesh, PartitionSpec as P

ROWS, COLS = ("y", "xh"), ("xl", "z", "c")
ALL = ROWS + COLS
N = 8


def device(y, xh, xl, z, core):
    return (((y * 2 + xh) * 2 + xl) * N + z) * 2 + core


CHIPS = [(y, xh, xl, z) for y in range(N) for xh in (0, 1) for xl in (0, 1) for z in range(N)]


def column_of(y, xh):
    return y // 4, (y % 4) * 2 + xh


def hidden_z(y, xh, token_y):
    return (column_of(y, xh)[1] + token_y - y) % N


def token_place(y, parity, token_y):
    return parity, (column_of(y, parity)[1] + token_y - y) % N


WIDE = [
    [device(y, xh, *token_place(y, xh ^ rel, a), 0) for rel in (0, 1) for a in range(N)]
    for y in range(N)
    for xh in (0, 1)
] + [
    [device(a, xl ^ rel, xl, z, 1) for rel in (0, 1) for a in range(N)] for xl in (0, 1) for z in range(N)
]
NARROW = [[device(a, xh, xl, z, 0) for a in range(N)] for xh in (0, 1) for xl in (0, 1) for z in range(N)] + [
    [device(y, xh, xl, hidden_z(y, xh, a), 1) for a in range(N)] for y in range(N) for xh in (0, 1) for xl in (0, 1)
]

SWAP = [(d, d ^ 1) for d in range(4 * N * N * 2)]
PARTNER = [(device(y, xh, xl, z, 0), device(y, 1 - xh, xl, z, 0)) for y, xh, xl, z in CHIPS] + [
    (device(y, xh, xl, z, 1), device(y, xh, 1 - xl, z, 1)) for y, xh, xl, z in CHIPS
]


def spread(core):
    moves = []
    for y, xh, xl, z in CHIPS:
        column = xl * N + z
        row = column // 2
        moves.append((device(y, xh, xl, z, core), device(row, xh, *token_place(row, column % 2, y), 0)))
        moves.append((device(y, xh, xl, z, 1 - core), device(y, xl, xh, z, 1)))
    return moves


SPREAD_OWN, SPREAD_OTHER = spread(0), spread(1)
CROSS = [
    move
    for y, xh, xl, z in CHIPS
    for a in [(z - column_of(y, xh)[1] + y) % N]
    for here, there in [(device(y, xh, xl, z, 1), device(a, xl, *column_of(y, xh), 0))]
    for move in ((here, there), (there, here))
]
BACK_OWN = [(device(y, xh, xl, z, core), device(y, xl, xh, z, core)) for y, xh, xl, z in CHIPS for core in (0, 1)]
BACK_OTHER = [(device(y, xh, xl, z, core), device(y, xl, xh, z, 1 - core)) for y, xh, xl, z in CHIPS for core in (0, 1)]


def trade(blocks, groups):
    return lax.all_to_all(blocks, ALL, split_axis=0, concat_axis=0, axis_index_groups=groups, tiled=True)


def gather(block, groups):
    return trade(jnp.broadcast_to(block, (len(groups[0]),) + block.shape), groups)


def reduce(partial, groups):
    return jnp.sum(trade(partial.astype(jnp.bfloat16), groups).astype(jnp.float32), axis=0)


def fold(wide):
    half = wide.shape[1] // 2
    return jnp.concatenate([wide[:, :half], wide[:, half:]], axis=0)


def unfold(tall):
    half = tall.shape[0] // 2
    return jnp.concatenate([tall[:half], tall[half:]], axis=1)


def local(tokens, mixer_out, gate_weight, out_weight, out_grad):
    f32, bf16 = jnp.float32, jnp.bfloat16
    first = lax.axis_index("c") == 0
    inner, width = gate_weight.shape[1], out_grad.shape[1]
    own = lax.ppermute(jnp.where(first, tokens, out_grad), ALL, SPREAD_OWN)
    other = lax.ppermute(jnp.where(first, out_grad, tokens), ALL, SPREAD_OTHER)
    acts = gather(jnp.concatenate([own, other], axis=1), WIDE)
    acts = acts.reshape(2, N * acts.shape[1], acts.shape[2])

    out_t = out_weight.T
    weight_in = lax.ppermute(jnp.where(first, fold(out_t), gate_weight), ALL, SWAP)
    weight = jnp.where(
        first,
        jnp.concatenate([gate_weight, weight_in], axis=1),
        jnp.concatenate([out_t, unfold(weight_in)], axis=0),
    )
    weight = jnp.stack([weight, lax.ppermute(weight, ALL, PARTNER)])
    mixer_in = lax.ppermute(mixer_out, ALL, SWAP)
    mixer_vals = jnp.concatenate([mixer_out, mixer_in], axis=1).astype(f32)

    partial = jnp.einsum("kad,kdn->an", acts, weight, preferred_element_type=f32)
    total = reduce(partial.reshape(N, -1, partial.shape[1]), NARROW)

    gate_pre = total
    gate_sig = jax.nn.sigmoid(gate_pre)
    gate_silu = gate_pre * gate_sig
    gated = (mixer_vals * gate_silu).astype(bf16)
    crossed = lax.ppermute(jnp.where(first, gated.astype(f32), total), ALL, CROSS)
    hidden_grad = crossed
    mixer_grad = (hidden_grad * gate_silu).astype(bf16)
    pre_grad = (hidden_grad * mixer_vals * gate_sig * (1.0 + gate_pre * (1.0 - gate_sig))).astype(bf16)
    units = gather(jnp.where(first, pre_grad, crossed.astype(bf16)), NARROW)
    units = units.reshape(-1, units.shape[2])

    layer_part = jnp.einsum("an,kdn->kad", units, weight, preferred_element_type=f32)
    layer_pair = reduce(layer_part.reshape(2 * N, -1, layer_part.shape[2]), WIDE).astype(bf16)
    layer_own = lax.ppermute(layer_pair[:, :width], ALL, BACK_OWN)
    layer_other = lax.ppermute(layer_pair[:, width:], ALL, BACK_OTHER)

    grads = jnp.einsum("kad,an->kdn", acts, units, preferred_element_type=f32)
    grads_in = lax.ppermute(grads[1].astype(bf16), ALL, PARTNER)
    grads = (grads[0] + grads_in.astype(f32)).astype(bf16)

    mixer_grad_in = lax.ppermute(mixer_grad[:, inner:], ALL, SWAP)
    grads_in = lax.ppermute(jnp.where(first, grads[:, inner:], fold(grads[width:])), ALL, SWAP)
    return (
        jnp.where(first, layer_other, layer_own),
        jnp.where(first, mixer_grad[:, :inner], mixer_grad_in),
        jnp.where(first, grads[:, :inner], grads_in),
        jnp.where(first, unfold(grads_in), grads[:width]).T,
    )


def solution(mesh):
    fine = Mesh(mesh.devices.reshape(N, 2, 2, N, 2), ALL)
    spec = P(ROWS, COLS)
    return jax.shard_map(local, mesh=fine, in_specs=(spec,) * 5, out_specs=(spec,) * 4, check_vma=False)
```

```python
import jax
import jax.numpy as jnp
from jax import lax
from jax.sharding import Mesh, PartitionSpec as P

ROWS, COLS = ("y", "xh"), ("xl", "z", "c")
ALL = ROWS + COLS
N = 8


def device(y, xh, xl, z, core):
    return (((y * 2 + xh) * 2 + xl) * N + z) * 2 + core


CHIPS = [(y, xh, xl, z) for y in range(N) for xh in (0, 1) for xl in (0, 1) for z in range(N)]


def column_of(y, xh):
    return y // 4, (y % 4) * 2 + xh


def hidden_z(y, xh, token_y):
    return (column_of(y, xh)[1] + token_y - y + N // 2) % N


def token_place(y, parity, token_y):
    return parity, (column_of(y, parity)[1] + token_y - y + N // 2) % N


WIDE = [
    [device(y, xh, *token_place(y, xh ^ rel, a), 0) for rel in (0, 1) for a in range(N)]
    for y in range(N)
    for xh in (0, 1)
] + [
    [device(a, xl ^ rel, xl, z, 1) for rel in (0, 1) for a in range(N)] for xl in (0, 1) for z in range(N)
]
NARROW = [[device(a, xh, xl, z, 0) for a in range(N)] for xh in (0, 1) for xl in (0, 1) for z in range(N)] + [
    [device(y, xh, xl, hidden_z(y, xh, a), 1) for a in range(N)] for y in range(N) for xh in (0, 1) for xl in (0, 1)
]

SWAP = [(d, d ^ 1) for d in range(4 * N * N * 2)]
PARTNER = [(device(y, xh, xl, z, 0), device(y, 1 - xh, xl, z, 0)) for y, xh, xl, z in CHIPS] + [
    (device(y, xh, xl, z, 1), device(y, xh, 1 - xl, z, 1)) for y, xh, xl, z in CHIPS
]
PARTNER_SWAP = [(device(y, xh, xl, z, 1), device(y, 1 - xh, xl, z, 0)) for y, xh, xl, z in CHIPS] + [
    (device(y, xh, xl, z, 0), device(y, xh, 1 - xl, z, 1)) for y, xh, xl, z in CHIPS
]


def spread(core):
    moves = []
    for y, xh, xl, z in CHIPS:
        column = xl * N + z
        row = column // 2
        moves.append((device(y, xh, xl, z, core), device(row, xh, *token_place(row, column % 2, y), 0)))
        moves.append((device(y, xh, xl, z, 1 - core), device(y, xl, xh, z, 1)))
    return moves


SPREAD_OWN, SPREAD_OTHER = spread(0), spread(1)
CROSS = [
    move
    for y, xh, xl, z in CHIPS
    for a in [(z - column_of(y, xh)[1] + y + N // 2) % N]
    for here, there in [(device(y, xh, xl, z, 1), device(a, xl, *column_of(y, xh), 0))]
    for move in ((here, there), (there, here))
]
BACK_OWN = [(device(y, xh, xl, z, core), device(y, xl, xh, z, core)) for y, xh, xl, z in CHIPS for core in (0, 1)]
BACK_OTHER = [(device(y, xh, xl, z, core), device(y, xl, xh, z, 1 - core)) for y, xh, xl, z in CHIPS for core in (0, 1)]


def trade(blocks, groups):
    return lax.all_to_all(blocks, ALL, split_axis=0, concat_axis=0, axis_index_groups=groups, tiled=True)


def gather(block, groups):
    return trade(jnp.broadcast_to(block, (len(groups[0]),) + block.shape), groups)


def reduce(partial, groups):
    return jnp.sum(trade(partial.astype(jnp.bfloat16), groups).astype(jnp.float32), axis=0)


def fold(wide):
    half = wide.shape[1] // 2
    return jnp.concatenate([wide[:, :half], wide[:, half:]], axis=0)


def unfold(tall):
    half = tall.shape[0] // 2
    return jnp.concatenate([tall[:half], tall[half:]], axis=1)


def local(tokens, mixer_out, gate_weight, out_weight, out_grad):
    f32, bf16 = jnp.float32, jnp.bfloat16
    first = lax.axis_index("c") == 0
    inner, width = gate_weight.shape[1], out_grad.shape[1]
    own = lax.ppermute(jnp.where(first, tokens, out_grad), ALL, SPREAD_OWN)
    other = lax.ppermute(jnp.where(first, out_grad, tokens), ALL, SPREAD_OTHER)
    acts = gather(jnp.concatenate([own, other], axis=1), WIDE)
    acts = acts.reshape(2, N * acts.shape[1], acts.shape[2])

    out_t = out_weight.T
    mine = jnp.where(first, gate_weight, fold(out_t))
    yours = jnp.where(first, fold(out_t), gate_weight)
    blocks = [
        (mine, lax.ppermute(yours, ALL, SWAP)),
        (lax.ppermute(mine, ALL, PARTNER), lax.ppermute(yours, ALL, PARTNER_SWAP)),
    ]
    weight = jnp.stack(
        [
            jnp.where(
                first,
                jnp.concatenate(pair, axis=1),
                jnp.concatenate([unfold(block) for block in pair], axis=0),
            )
            for pair in blocks
        ]
    )
    mixer_in = lax.ppermute(mixer_out, ALL, SWAP)
    mixer_vals = jnp.concatenate([mixer_out, mixer_in], axis=1).astype(f32)

    partial = jnp.einsum("kad,kdn->an", acts, weight, preferred_element_type=f32)
    total = reduce(partial.reshape(N, -1, partial.shape[1]), NARROW)

    gate_pre = total
    gate_sig = jax.nn.sigmoid(gate_pre)
    gate_silu = gate_pre * gate_sig
    gated = (mixer_vals * gate_silu).astype(bf16)
    crossed = lax.ppermute(jnp.where(first, gated, total.astype(bf16)), ALL, CROSS)
    hidden_grad = crossed.astype(f32)
    mixer_grad = (hidden_grad * gate_silu).astype(bf16)
    pre_grad = (hidden_grad * mixer_vals * gate_sig * (1.0 + gate_pre * (1.0 - gate_sig))).astype(bf16)
    units = gather(jnp.where(first, pre_grad, crossed), NARROW)
    mixer_grad_in = lax.ppermute(mixer_grad[:, inner:], ALL, SWAP)
    units, mixer_grad_in = lax.optimization_barrier((units, mixer_grad_in))
    units = units.reshape(-1, units.shape[2])

    grads = jnp.einsum("kad,an->kdn", acts, units, preferred_element_type=f32)
    units, grads_out = lax.optimization_barrier((units, grads[1].astype(bf16)))
    grads_in = lax.ppermute(grads_out, ALL, PARTNER)

    layer_part = jnp.einsum("an,kdn->kad", units, weight, preferred_element_type=f32)
    layer_pair = reduce(layer_part.reshape(2 * N, -1, layer_part.shape[2]), WIDE).astype(bf16)
    layer_own = lax.ppermute(layer_pair[:, :width], ALL, BACK_OWN)
    layer_other = lax.ppermute(layer_pair[:, width:], ALL, BACK_OTHER)

    grads = (grads[0] + grads_in.astype(f32)).astype(bf16)
    grads_in = lax.ppermute(jnp.where(first, grads[:, inner:], fold(grads[width:])), ALL, SWAP)
    return (
        jnp.where(first, layer_other, layer_own),
        jnp.where(first, mixer_grad[:, :inner], mixer_grad_in),
        jnp.where(first, grads[:, :inner], grads_in),
        jnp.where(first, unfold(grads_in), grads[:width]).T,
    )


def solution(mesh):
    fine = Mesh(mesh.devices.reshape(N, 2, 2, N, 2), ALL)
    spec = P(ROWS, COLS)
    return jax.shard_map(local, mesh=fine, in_specs=(spec,) * 5, out_specs=(spec,) * 4, check_vma=False)
```

```python
import jax
import jax.numpy as jnp
from jax import lax
from jax.sharding import Mesh, PartitionSpec as P

ROWS, COLS = ("y", "xh"), ("xl", "z", "c")
ALL = ROWS + COLS
N = 8


def device(y, xh, xl, z, core):
    return (((y * 2 + xh) * 2 + xl) * N + z) * 2 + core


CHIPS = [(y, xh, xl, z) for y in range(N) for xh in (0, 1) for xl in (0, 1) for z in range(N)]


def column_of(y, xh):
    return y // 4, (y % 4) * 2 + xh


def hidden_z(y, xh, token_y):
    return (column_of(y, xh)[1] + token_y - y + N // 2) % N


def token_place(y, parity, token_y):
    return parity, (column_of(y, parity)[1] + token_y - y + N // 2) % N


WIDE = [
    [device(y, xh, *token_place(y, xh ^ rel, a), 0) for rel in (0, 1) for a in range(N)]
    for y in range(N)
    for xh in (0, 1)
] + [
    [device(a, xl ^ rel, xl, z, 1) for rel in (0, 1) for a in range(N)] for xl in (0, 1) for z in range(N)
]
NARROW = [[device(a, xh, xl, z, 0) for a in range(N)] for xh in (0, 1) for xl in (0, 1) for z in range(N)] + [
    [device(y, xh, xl, hidden_z(y, xh, a), 1) for a in range(N)] for y in range(N) for xh in (0, 1) for xl in (0, 1)
]

SWAP = [(d, d ^ 1) for d in range(4 * N * N * 2)]
PARTNER = [(device(y, xh, xl, z, 0), device(y, 1 - xh, xl, z, 0)) for y, xh, xl, z in CHIPS] + [
    (device(y, xh, xl, z, 1), device(y, xh, 1 - xl, z, 1)) for y, xh, xl, z in CHIPS
]
PARTNER_SWAP = [(device(y, xh, xl, z, 1), device(y, 1 - xh, xl, z, 0)) for y, xh, xl, z in CHIPS] + [
    (device(y, xh, xl, z, 0), device(y, xh, 1 - xl, z, 1)) for y, xh, xl, z in CHIPS
]
SWAP_PARTNER = [(there, here) for here, there in PARTNER_SWAP]


def spread(core):
    moves = []
    for y, xh, xl, z in CHIPS:
        column = xl * N + z
        row = column // 2
        moves.append((device(y, xh, xl, z, core), device(row, xh, *token_place(row, column % 2, y), 0)))
        moves.append((device(y, xh, xl, z, 1 - core), device(y, xl, xh, z, 1)))
    return moves


SPREAD_OWN, SPREAD_OTHER = spread(0), spread(1)
CROSS = [
    move
    for y, xh, xl, z in CHIPS
    for a in [(z - column_of(y, xh)[1] + y + N // 2) % N]
    for here, there in [(device(y, xh, xl, z, 1), device(a, xl, *column_of(y, xh), 0))]
    for move in ((here, there), (there, here))
]
BACK_OWN = [(device(y, xh, xl, z, core), device(y, xl, xh, z, core)) for y, xh, xl, z in CHIPS for core in (0, 1)]
BACK_OTHER = [(device(y, xh, xl, z, core), device(y, xl, xh, z, 1 - core)) for y, xh, xl, z in CHIPS for core in (0, 1)]


def trade(blocks, groups):
    return lax.all_to_all(blocks, ALL, split_axis=0, concat_axis=0, axis_index_groups=groups, tiled=True)


def gather(block, groups):
    return trade(jnp.broadcast_to(block, (len(groups[0]),) + block.shape), groups)


def reduce(partial, groups):
    return jnp.sum(trade(partial.astype(jnp.bfloat16), groups).astype(jnp.float32), axis=0)


def fold(wide):
    half = wide.shape[1] // 2
    return jnp.concatenate([wide[:, :half], wide[:, half:]], axis=0)


def unfold(tall):
    half = tall.shape[0] // 2
    return jnp.concatenate([tall[:half], tall[half:]], axis=1)


def local(tokens, mixer_out, gate_weight, out_weight, out_grad):
    f32, bf16 = jnp.float32, jnp.bfloat16
    first = lax.axis_index("c") == 0
    inner, width = gate_weight.shape[1], out_grad.shape[1]
    own = lax.ppermute(jnp.where(first, tokens, out_grad), ALL, SPREAD_OWN)
    other = lax.ppermute(jnp.where(first, out_grad, tokens), ALL, SPREAD_OTHER)
    out_t = out_weight.T
    mine = jnp.where(first, gate_weight, fold(out_t))
    yours = jnp.where(first, fold(out_t), gate_weight)
    weights_in = [lax.ppermute(yours, ALL, SWAP), lax.ppermute(mine, ALL, PARTNER), lax.ppermute(yours, ALL, PARTNER_SWAP)]
    acts = gather(jnp.concatenate([own, other], axis=1), WIDE)
    mixer_in = lax.ppermute(mixer_out, ALL, SWAP)
    acts, mixer_in = lax.optimization_barrier((acts, mixer_in))
    acts = acts.reshape(2, N * acts.shape[1], acts.shape[2])
    blocks = [(mine, weights_in[0]), weights_in[1:]]
    weight = jnp.stack(
        [
            jnp.where(
                first,
                jnp.concatenate(pair, axis=1),
                jnp.concatenate([unfold(block) for block in pair], axis=0),
            )
            for pair in blocks
        ]
    )
    mixer_vals = jnp.concatenate([mixer_out, mixer_in], axis=1).astype(f32)

    partial = jnp.einsum("kad,kdn->an", acts, weight, preferred_element_type=f32)
    total = reduce(partial.reshape(N, -1, partial.shape[1]), NARROW)

    gate_pre = total
    gate_sig = jax.nn.sigmoid(gate_pre)
    gate_silu = gate_pre * gate_sig
    gated = (mixer_vals * gate_silu).astype(bf16)
    crossed = lax.ppermute(jnp.where(first, gated, total.astype(bf16)), ALL, CROSS)
    hidden_grad = crossed.astype(f32)
    mixer_grad = (hidden_grad * gate_silu).astype(bf16)
    pre_grad = (hidden_grad * mixer_vals * gate_sig * (1.0 + gate_pre * (1.0 - gate_sig))).astype(bf16)
    units = gather(jnp.where(first, pre_grad, crossed), NARROW)
    mixer_grad_in = lax.ppermute(mixer_grad[:, inner:], ALL, SWAP)
    units, mixer_grad_in = lax.optimization_barrier((units, mixer_grad_in))
    units = units.reshape(-1, units.shape[2])

    layer_part = jnp.einsum("an,kdn->kad", units, weight, preferred_element_type=f32)
    layer_pair = reduce(layer_part.reshape(2 * N, -1, layer_part.shape[2]), WIDE).astype(bf16)

    grads = jnp.einsum("kad,an->kdn", acts, units, preferred_element_type=f32)
    keep = jnp.where(first, grads[:, :, :inner], jnp.stack([fold(g) for g in grads[:, :width]]))
    send = jnp.where(first, grads[:, :, inner:], jnp.stack([fold(g) for g in grads[:, width:]]))
    swap_in = lax.ppermute(send[0], ALL, SWAP)
    keep_far, send_far = keep[1].astype(bf16), send[1].astype(bf16)
    layer_own = lax.ppermute(layer_pair[:, :width], ALL, BACK_OWN)
    layer_other = lax.ppermute(layer_pair[:, width:], ALL, BACK_OTHER)
    kept = (keep[0] + lax.ppermute(keep_far, ALL, PARTNER).astype(f32)).astype(bf16)
    sent = (swap_in + lax.ppermute(send_far, ALL, SWAP_PARTNER).astype(f32)).astype(bf16)
    return (
        jnp.where(first, layer_other, layer_own),
        jnp.where(first, mixer_grad[:, :inner], mixer_grad_in),
        jnp.where(first, kept, sent),
        unfold(jnp.where(first, sent, kept)).T,
    )


def solution(mesh):
    fine = Mesh(mesh.devices.reshape(N, 2, 2, N, 2), ALL)
    spec = P(ROWS, COLS)
    return jax.shard_map(local, mesh=fine, in_specs=(spec,) * 5, out_specs=(spec,) * 4, check_vma=False)
```

```python
import jax
import jax.numpy as jnp
from jax import lax
from jax.sharding import Mesh, PartitionSpec as P

ROWS, COLS = ("y", "xh"), ("xl", "z", "c")
ALL = ROWS + COLS
N = 8


def device(y, xh, xl, z, core):
    return (((y * 2 + xh) * 2 + xl) * N + z) * 2 + core


CHIPS = [(y, xh, xl, z) for y in range(N) for xh in (0, 1) for xl in (0, 1) for z in range(N)]


def column_of(y, xh):
    return y // 4, (y % 4) * 2 + xh


def hidden_z(y, xh, token_y):
    return (column_of(y, xh)[1] + token_y - y + N // 2) % N


def token_place(y, parity, token_y):
    return parity, (column_of(y, parity)[1] + token_y - y + N // 2) % N


WIDE = [
    [device(y, xh, *token_place(y, xh ^ rel, a), 0) for rel in (0, 1) for a in range(N)]
    for y in range(N)
    for xh in (0, 1)
] + [
    [device(a, xl ^ rel, xl, z, 1) for rel in (0, 1) for a in range(N)] for xl in (0, 1) for z in range(N)
]
NARROW = [[device(a, xh, xl, z, 0) for a in range(N)] for xh in (0, 1) for xl in (0, 1) for z in range(N)] + [
    [device(y, xh, xl, hidden_z(y, xh, a), 1) for a in range(N)] for y in range(N) for xh in (0, 1) for xl in (0, 1)
]

SWAP = [(d, d ^ 1) for d in range(4 * N * N * 2)]
PARTNER = [(device(y, xh, xl, z, 0), device(y, 1 - xh, xl, z, 0)) for y, xh, xl, z in CHIPS] + [
    (device(y, xh, xl, z, 1), device(y, xh, 1 - xl, z, 1)) for y, xh, xl, z in CHIPS
]
PARTNER_SWAP = [(device(y, xh, xl, z, 1), device(y, 1 - xh, xl, z, 0)) for y, xh, xl, z in CHIPS] + [
    (device(y, xh, xl, z, 0), device(y, xh, 1 - xl, z, 1)) for y, xh, xl, z in CHIPS
]
SWAP_PARTNER = [(there, here) for here, there in PARTNER_SWAP]


def spread(core):
    moves = []
    for y, xh, xl, z in CHIPS:
        column = xl * N + z
        row = column // 2
        moves.append((device(y, xh, xl, z, core), device(row, xh, *token_place(row, column % 2, y), 0)))
        moves.append((device(y, xh, xl, z, 1 - core), device(y, xl, xh, z, 1)))
    return moves


SPREAD_OWN, SPREAD_OTHER = spread(0), spread(1)
CROSS = [
    move
    for y, xh, xl, z in CHIPS
    for a in [(z - column_of(y, xh)[1] + y + N // 2) % N]
    for here, there in [(device(y, xh, xl, z, 1), device(a, xl, *column_of(y, xh), 0))]
    for move in ((here, there), (there, here))
]
BACK_OWN = [(device(y, xh, xl, z, core), device(y, xl, xh, z, core)) for y, xh, xl, z in CHIPS for core in (0, 1)]
BACK_OTHER = [(device(y, xh, xl, z, core), device(y, xl, xh, z, 1 - core)) for y, xh, xl, z in CHIPS for core in (0, 1)]


def trade(blocks, groups):
    return lax.all_to_all(blocks, ALL, split_axis=0, concat_axis=0, axis_index_groups=groups, tiled=True)


def gather(block, groups):
    return trade(jnp.broadcast_to(block, (len(groups[0]),) + block.shape), groups)


def reduce(partial, groups):
    return jnp.sum(trade(partial.astype(jnp.bfloat16), groups).astype(jnp.float32), axis=0)


def fold(wide):
    half = wide.shape[1] // 2
    return jnp.concatenate([wide[:, :half], wide[:, half:]], axis=0)


def unfold(tall):
    half = tall.shape[0] // 2
    return jnp.concatenate([tall[:half], tall[half:]], axis=1)


def local(tokens, mixer_out, gate_weight, out_weight, out_grad):
    f32, bf16 = jnp.float32, jnp.bfloat16
    first = lax.axis_index("c") == 0
    inner, width = gate_weight.shape[1], out_grad.shape[1]
    own = lax.ppermute(jnp.where(first, tokens, out_grad), ALL, SPREAD_OWN)
    other = lax.ppermute(jnp.where(first, out_grad, tokens), ALL, SPREAD_OTHER)
    out_t = out_weight.T
    mine = jnp.where(first, gate_weight, fold(out_t))
    yours = jnp.where(first, fold(out_t), gate_weight)
    own, other, swapped = lax.optimization_barrier((own, other, lax.ppermute(yours, ALL, SWAP)))
    acts = gather(jnp.concatenate([own, other], axis=1), WIDE)
    mixer_in = lax.ppermute(mixer_out, ALL, SWAP)
    acts, mixer_in = lax.optimization_barrier((acts, mixer_in))
    acts = acts.reshape(2, N * acts.shape[1], acts.shape[2])
    weight = jnp.where(
        first,
        jnp.concatenate([mine, swapped], axis=1),
        jnp.concatenate([unfold(mine), unfold(swapped)], axis=0),
    )
    weight = jnp.stack([weight, lax.ppermute(weight, ALL, PARTNER)])
    mixer_vals = jnp.concatenate([mixer_out, mixer_in], axis=1).astype(f32)

    partial = jnp.einsum("kad,kdn->an", acts, weight, preferred_element_type=f32)
    total = reduce(partial.reshape(N, -1, partial.shape[1]), NARROW)

    gate_pre = total
    gate_sig = jax.nn.sigmoid(gate_pre)
    gate_silu = gate_pre * gate_sig
    gated = (mixer_vals * gate_silu).astype(bf16)
    crossed = lax.ppermute(jnp.where(first, gated, total.astype(bf16)), ALL, CROSS)
    hidden_grad = crossed.astype(f32)
    mixer_grad = (hidden_grad * gate_silu).astype(bf16)
    pre_grad = (hidden_grad * mixer_vals * gate_sig * (1.0 + gate_pre * (1.0 - gate_sig))).astype(bf16)
    units = gather(jnp.where(first, pre_grad, crossed), NARROW)
    mixer_grad_in = lax.ppermute(mixer_grad[:, inner:], ALL, SWAP)
    units, mixer_grad_in = lax.optimization_barrier((units, mixer_grad_in))
    units = units.reshape(-1, units.shape[2])

    parts = [lax.dot_general(units, w, (((1,), (1,)), ((), ())), preferred_element_type=f32).astype(bf16) for w in weight]
    layer_part, units = lax.optimization_barrier((jnp.stack(parts), units))
    layer_pair = reduce(layer_part.reshape(2 * N, -1, layer_part.shape[2]), WIDE).astype(bf16)

    grads = jnp.einsum("kad,an->kdn", acts, units, preferred_element_type=f32)
    keep = jnp.where(first, grads[:, :, :inner], jnp.stack([fold(g) for g in grads[:, :width]]))
    send = jnp.where(first, grads[:, :, inner:], jnp.stack([fold(g) for g in grads[:, width:]]))
    swap_in = lax.ppermute(send[0], ALL, SWAP)
    keep_far, send_far = keep[1].astype(bf16), send[1].astype(bf16)
    layer_own = lax.ppermute(layer_pair[:, :width], ALL, BACK_OWN)
    layer_other = lax.ppermute(layer_pair[:, width:], ALL, BACK_OTHER)
    kept = (keep[0] + lax.ppermute(keep_far, ALL, PARTNER).astype(f32)).astype(bf16)
    sent = (swap_in + lax.ppermute(send_far, ALL, SWAP_PARTNER).astype(f32)).astype(bf16)
    return (
        jnp.where(first, layer_other, layer_own),
        jnp.where(first, mixer_grad[:, :inner], mixer_grad_in),
        jnp.where(first, kept, sent),
        unfold(jnp.where(first, sent, kept)).T,
    )


def solution(mesh):
    fine = Mesh(mesh.devices.reshape(N, 2, 2, N, 2), ALL)
    spec = P(ROWS, COLS)
    return jax.shard_map(local, mesh=fine, in_specs=(spec,) * 5, out_specs=(spec,) * 4, check_vma=False)
```

```python
import jax
import jax.numpy as jnp
from jax import lax
from jax.sharding import Mesh, PartitionSpec as P

ROWS, COLS = ("y", "xh"), ("xl", "z", "c")
ALL = ROWS + COLS
N = 8


def device(y, xh, xl, z, core):
    return (((y * 2 + xh) * 2 + xl) * N + z) * 2 + core


CHIPS = [(y, xh, xl, z) for y in range(N) for xh in (0, 1) for xl in (0, 1) for z in range(N)]


def column_of(y, xh):
    return y // 4, (y % 4) * 2 + xh


def hidden_z(y, xh, token_y):
    return (column_of(y, xh)[1] + token_y - y + N // 2) % N


def token_place(y, parity, token_y):
    return parity, (column_of(y, parity)[1] + token_y - y + N // 2) % N


WIDE = [
    [device(y, xh, *token_place(y, xh ^ rel, a), 0) for rel in (0, 1) for a in range(N)]
    for y in range(N)
    for xh in (0, 1)
] + [
    [device(a, xl ^ rel, xl, z, 1) for rel in (0, 1) for a in range(N)] for xl in (0, 1) for z in range(N)
]
ROW_GROUPS = [
    [device(a, xl ^ rel, xl, z, core) for rel in (0, 1) for a in range(N)]
    for core in (0, 1)
    for xl in (0, 1)
    for z in range(N)
]
NARROW = [[device(a, xh, xl, z, 0) for a in range(N)] for xh in (0, 1) for xl in (0, 1) for z in range(N)] + [
    [device(y, xh, xl, hidden_z(y, xh, a), 1) for a in range(N)] for y in range(N) for xh in (0, 1) for xl in (0, 1)
]

SWAP = [(d, d ^ 1) for d in range(4 * N * N * 2)]
PARTNER = [(device(y, xh, xl, z, 0), device(y, 1 - xh, xl, z, 0)) for y, xh, xl, z in CHIPS] + [
    (device(y, xh, xl, z, 1), device(y, xh, 1 - xl, z, 1)) for y, xh, xl, z in CHIPS
]
PARTNER_SWAP = [(device(y, xh, xl, z, 1), device(y, 1 - xh, xl, z, 0)) for y, xh, xl, z in CHIPS] + [
    (device(y, xh, xl, z, 0), device(y, xh, 1 - xl, z, 1)) for y, xh, xl, z in CHIPS
]
SWAP_PARTNER = [(there, here) for here, there in PARTNER_SWAP]


def spread(core):
    moves = []
    for y, xh, xl, z in CHIPS:
        column = xl * N + z
        row = column // 2
        moves.append((device(y, xh, xl, z, core), device(row, xh, *token_place(row, column % 2, y), 0)))
        moves.append((device(y, xh, xl, z, 1 - core), device(y, xl, xh, z, 1)))
    return moves


SPREAD_OWN, SPREAD_OTHER = spread(0), spread(1)
CROSS = [
    move
    for y, xh, xl, z in CHIPS
    for a in [(z - column_of(y, xh)[1] + y + N // 2) % N]
    for here, there in [(device(y, xh, xl, z, 1), device(a, xl, *column_of(y, xh), 0))]
    for move in ((here, there), (there, here))
]
BACK = [(device(y, xh, xl, z, core), device(y, xl, xh, z, core)) for y, xh, xl, z in CHIPS for core in (0, 1)]


def trade(blocks, groups):
    return lax.all_to_all(blocks, ALL, split_axis=0, concat_axis=0, axis_index_groups=groups, tiled=True)


def gather(block, groups):
    return trade(jnp.broadcast_to(block, (len(groups[0]),) + block.shape), groups)


def reduce(partial, groups):
    return jnp.sum(trade(partial.astype(jnp.bfloat16), groups).astype(jnp.float32), axis=0)


def fold(tall):
    half = tall.shape[0] // 2
    return jnp.concatenate([tall[:half], tall[half:]], axis=1)


def unfold(block):
    half = block.shape[1] // 2
    return jnp.concatenate([block[:, :half], block[:, half:]], axis=0)


def wide_fold(wide):
    half = wide.shape[2] // 2
    return jnp.concatenate([wide[:, :, :half], wide[:, :, half:]], axis=1)


def wide_unfold(block):
    half = block.shape[0] // 2
    return jnp.concatenate([block[:half], block[half:]], axis=1)


def local(tokens, mixer_out, gate_weight, out_weight, out_grad):
    f32, bf16 = jnp.float32, jnp.bfloat16
    first = lax.axis_index("c") == 0
    inner, width = gate_weight.shape[1], out_grad.shape[1]
    own = lax.ppermute(jnp.where(first, tokens, out_grad), ALL, SPREAD_OWN)
    other = lax.ppermute(jnp.where(first, out_grad, tokens), ALL, SPREAD_OTHER)
    mine = jnp.where(first, gate_weight, fold(out_weight))
    yours = jnp.where(first, fold(out_weight), gate_weight)
    swapped = lax.ppermute(yours, ALL, SWAP)
    own, other, mine, swapped = lax.optimization_barrier((own, other, mine, swapped))
    acts = gather(jnp.concatenate([own, other], axis=1), WIDE)
    mixer_in = lax.ppermute(mixer_out, ALL, SWAP)
    acts, mixer_in = lax.optimization_barrier((acts, mixer_in))
    acts = acts.reshape(2, N * acts.shape[1], acts.shape[2])
    weight = jnp.where(
        first,
        jnp.concatenate([mine, swapped], axis=1),
        jnp.concatenate([unfold(mine), unfold(swapped)], axis=1).T,
    )
    weight = jnp.stack([weight, lax.ppermute(weight, ALL, PARTNER)])
    mixer_vals = jnp.concatenate([mixer_out, mixer_in], axis=1).astype(f32)

    partial = jnp.einsum("kad,kdn->an", acts, weight, preferred_element_type=f32)
    total = reduce(partial.reshape(N, -1, partial.shape[1]), NARROW)

    gate_pre = total
    gate_sig = jax.nn.sigmoid(gate_pre)
    gate_silu = gate_pre * gate_sig
    gated = (mixer_vals * gate_silu).astype(bf16)
    crossed = lax.ppermute(jnp.where(first, gated, total.astype(bf16)), ALL, CROSS)
    hidden_grad = crossed.astype(f32)
    mixer_grad = (hidden_grad * gate_silu).astype(bf16)
    pre_grad = (hidden_grad * mixer_vals * gate_sig * (1.0 + gate_pre * (1.0 - gate_sig))).astype(bf16)
    units = gather(jnp.where(first, pre_grad, crossed), NARROW)
    mixer_grad_in = lax.ppermute(mixer_grad[:, inner:], ALL, SWAP)
    units, mixer_grad_in = lax.optimization_barrier((units, mixer_grad_in))
    units = units.reshape(-1, units.shape[2])

    def layer_part(start):
        return jnp.stack(
            [
                lax.dot_general(
                    units, w[start : start + width], (((1,), (1,)), ((), ())), preferred_element_type=f32
                ).astype(bf16)
                for w in weight
            ]
        )

    layer_in = lax.ppermute(layer_part(width), ALL, SWAP)
    layer_blocks = jnp.where(first, layer_in, layer_part(0))
    layer_own = reduce(layer_blocks.reshape(2 * N, -1, width), ROW_GROUPS).astype(bf16)

    grads = jnp.einsum("kad,an->kdn", acts, units, preferred_element_type=f32)
    keep = jnp.where(first, grads[:, :, :inner], wide_fold(grads[:, :width]))
    send = jnp.where(first, grads[:, :, inner:], wide_fold(grads[:, width:]))
    swap_in = lax.ppermute(send[0], ALL, SWAP)
    keep_far, send_far = keep[1].astype(bf16), send[1].astype(bf16)
    layer_out = lax.ppermute(layer_own, ALL, BACK)
    kept = (keep[0] + lax.ppermute(keep_far, ALL, PARTNER).astype(f32)).astype(bf16)
    sent = (swap_in + lax.ppermute(send_far, ALL, SWAP_PARTNER).astype(f32)).astype(bf16)
    return (
        layer_out,
        jnp.where(first, mixer_grad[:, :inner], mixer_grad_in),
        jnp.where(first, kept, sent),
        wide_unfold(jnp.where(first, sent, kept)).T,
    )


def solution(mesh):
    fine = Mesh(mesh.devices.reshape(N, 2, 2, N, 2), ALL)
    spec = P(ROWS, COLS)
    return jax.shard_map(local, mesh=fine, in_specs=(spec,) * 5, out_specs=(spec,) * 4, check_vma=False)
```

```python
import jax
import jax.numpy as jnp
from jax import lax
from jax.experimental.layout import Layout, with_layout_constraint
from jax.sharding import Mesh, PartitionSpec as P

ROWS, COLS = ("y", "xh"), ("xl", "z", "c")
ALL = ROWS + COLS
BY_ROWS = Layout(major_to_minor=(0, 1))
N = 8


def device(y, xh, xl, z, core):
    return (((y * 2 + xh) * 2 + xl) * N + z) * 2 + core


CHIPS = [(y, xh, xl, z) for y in range(N) for xh in (0, 1) for xl in (0, 1) for z in range(N)]


def column_of(y, xh):
    return y // 4, (y % 4) * 2 + xh


def hidden_z(y, xh, token_y):
    return (column_of(y, xh)[1] + token_y - y + N // 2) % N


def token_place(y, parity, token_y):
    return parity, (column_of(y, parity)[1] + token_y - y + N // 2) % N


WIDE = [
    [device(y, xh, *token_place(y, xh ^ rel, a), 0) for rel in (0, 1) for a in range(N)]
    for y in range(N)
    for xh in (0, 1)
] + [
    [device(a, xl ^ rel, xl, z, 1) for rel in (0, 1) for a in range(N)] for xl in (0, 1) for z in range(N)
]
ROW_GROUPS = [
    [device(a, xl ^ rel, xl, z, core) for rel in (0, 1) for a in range(N)]
    for core in (0, 1)
    for xl in (0, 1)
    for z in range(N)
]
NARROW = [[device(a, xh, xl, z, 0) for a in range(N)] for xh in (0, 1) for xl in (0, 1) for z in range(N)] + [
    [device(y, xh, xl, hidden_z(y, xh, a), 1) for a in range(N)] for y in range(N) for xh in (0, 1) for xl in (0, 1)
]

SWAP = [(d, d ^ 1) for d in range(4 * N * N * 2)]
PARTNER = [(device(y, xh, xl, z, 0), device(y, 1 - xh, xl, z, 0)) for y, xh, xl, z in CHIPS] + [
    (device(y, xh, xl, z, 1), device(y, xh, 1 - xl, z, 1)) for y, xh, xl, z in CHIPS
]
PARTNER_SWAP = [(device(y, xh, xl, z, 1), device(y, 1 - xh, xl, z, 0)) for y, xh, xl, z in CHIPS] + [
    (device(y, xh, xl, z, 0), device(y, xh, 1 - xl, z, 1)) for y, xh, xl, z in CHIPS
]
SWAP_PARTNER = [(there, here) for here, there in PARTNER_SWAP]


def spread(core):
    moves = []
    for y, xh, xl, z in CHIPS:
        column = xl * N + z
        row = column // 2
        moves.append((device(y, xh, xl, z, core), device(row, xh, *token_place(row, column % 2, y), 0)))
        moves.append((device(y, xh, xl, z, 1 - core), device(y, xl, xh, z, 1)))
    return moves


SPREAD = spread(0)
CROSS = [
    move
    for y, xh, xl, z in CHIPS
    for a in [(z - column_of(y, xh)[1] + y + N // 2) % N]
    for here, there in [(device(y, xh, xl, z, 1), device(a, xl, *column_of(y, xh), 0))]
    for move in ((here, there), (there, here))
]
BACK = [(device(y, xh, xl, z, core), device(y, xl, xh, z, core)) for y, xh, xl, z in CHIPS for core in (0, 1)]


def trade(blocks, groups):
    return lax.all_to_all(blocks, ALL, split_axis=0, concat_axis=0, axis_index_groups=groups, tiled=True)


def gather(block, groups):
    return trade(jnp.broadcast_to(block, (len(groups[0]),) + block.shape), groups)


def reduce(partial, groups):
    return jnp.sum(trade(partial.astype(jnp.bfloat16), groups).astype(jnp.float32), axis=0)


def fold(block):
    half = block.shape[1] // 2
    return jnp.concatenate([block[:, :half], block[:, half:]], axis=0)


def unfold(tall):
    half = tall.shape[0] // 2
    return jnp.concatenate([tall[:half], tall[half:]], axis=1)


def wide_fold(wide):
    half = wide.shape[2] // 2
    return jnp.concatenate([wide[:, :, :half], wide[:, :, half:]], axis=1)


def wide_unfold(block):
    half = block.shape[0] // 2
    return jnp.concatenate([block[:half], block[half:]], axis=1)


def local(tokens, mixer_out, gate_weight, out_weight, out_grad):
    f32, bf16 = jnp.float32, jnp.bfloat16
    first = lax.axis_index("c") == 0
    inner, width = gate_weight.shape[1], out_grad.shape[1]
    mine = jnp.where(first, tokens, out_grad)
    yours = jnp.where(first, out_grad, tokens)
    block = jnp.where(first, out_weight, fold(gate_weight))
    sent = with_layout_constraint(jnp.concatenate([yours, block], axis=0), BY_ROWS)
    swapped = with_layout_constraint(lax.ppermute(sent, ALL, SWAP), BY_ROWS)
    pair = lax.ppermute(jnp.concatenate([mine, swapped[: mine.shape[0]]], axis=1), ALL, SPREAD)
    block = swapped[mine.shape[0] :]
    weight = jnp.where(
        first,
        jnp.concatenate([gate_weight, unfold(block)], axis=1),
        jnp.concatenate([out_weight, block], axis=1).T,
    )
    acts = gather(pair, WIDE)
    mixer_in = lax.ppermute(mixer_out, ALL, SWAP)
    acts, mixer_in = lax.optimization_barrier((acts, mixer_in))
    acts = acts.reshape(2, N * acts.shape[1], acts.shape[2])
    weight = jnp.stack([weight, lax.ppermute(weight, ALL, PARTNER)])
    mixer_vals = jnp.concatenate([mixer_out, mixer_in], axis=1).astype(f32)

    partial = jnp.einsum("kad,kdn->an", acts, weight, preferred_element_type=f32)
    total = reduce(partial.reshape(N, -1, partial.shape[1]), NARROW)

    gate_pre = total
    gate_sig = jax.nn.sigmoid(gate_pre)
    gate_silu = gate_pre * gate_sig
    gated = (mixer_vals * gate_silu).astype(bf16)
    crossed = lax.ppermute(jnp.where(first, gated, total.astype(bf16)), ALL, CROSS)
    hidden_grad = crossed.astype(f32)
    mixer_grad = (hidden_grad * gate_silu).astype(bf16)
    pre_grad = (hidden_grad * mixer_vals * gate_sig * (1.0 + gate_pre * (1.0 - gate_sig))).astype(bf16)
    units = gather(jnp.where(first, pre_grad, crossed), NARROW)
    mixer_grad_in = lax.ppermute(mixer_grad[:, inner:], ALL, SWAP)
    units, mixer_grad_in = lax.optimization_barrier((units, mixer_grad_in))
    units = units.reshape(-1, units.shape[2])

    def layer_part(start):
        return jnp.stack(
            [
                lax.dot_general(
                    units, w[start : start + width], (((1,), (1,)), ((), ())), preferred_element_type=f32
                ).astype(bf16)
                for w in weight
            ]
        )

    layer_in = lax.ppermute(layer_part(width), ALL, SWAP)
    layer_blocks = jnp.where(first, layer_in, layer_part(0))
    layer_own = reduce(layer_blocks.reshape(2 * N, -1, width), ROW_GROUPS).astype(bf16)

    grads = jnp.einsum("kad,an->kdn", acts, units, preferred_element_type=f32)
    keep = jnp.where(first, grads[:, :, :inner], wide_fold(grads[:, :width]))
    send = jnp.where(first, grads[:, :, inner:], wide_fold(grads[:, width:]))
    swap_in = lax.ppermute(send[0], ALL, SWAP)
    keep_far, send_far = keep[1].astype(bf16), send[1].astype(bf16)
    layer_out = lax.ppermute(layer_own, ALL, BACK)
    kept = (keep[0] + lax.ppermute(keep_far, ALL, PARTNER).astype(f32)).astype(bf16)
    sent = (swap_in + lax.ppermute(send_far, ALL, SWAP_PARTNER).astype(f32)).astype(bf16)
    return (
        layer_out,
        jnp.where(first, mixer_grad[:, :inner], mixer_grad_in),
        jnp.where(first, kept, sent),
        wide_unfold(jnp.where(first, sent, kept)).T,
    )


def solution(mesh):
    fine = Mesh(mesh.devices.reshape(N, 2, 2, N, 2), ALL)
    spec = P(ROWS, COLS)
    return jax.shard_map(local, mesh=fine, in_specs=(spec,) * 5, out_specs=(spec,) * 4, check_vma=False)
```

```python
import jax
import jax.numpy as jnp
from jax import lax
from jax.experimental.layout import Layout, with_layout_constraint
from jax.sharding import Mesh, PartitionSpec as P

ROWS, COLS = ("y", "xh"), ("xl", "z", "c")
ALL = ROWS + COLS
BY_ROWS = Layout(major_to_minor=(0, 1))
N = 8


def device(y, xh, xl, z, core):
    return (((y * 2 + xh) * 2 + xl) * N + z) * 2 + core


CHIPS = [(y, xh, xl, z) for y in range(N) for xh in (0, 1) for xl in (0, 1) for z in range(N)]


def column_of(y, xh):
    return y // 4, (y % 4) * 2 + xh


def hidden_z(y, xh, token_y):
    return (column_of(y, xh)[1] + token_y - y + N // 2) % N


def token_place(y, parity, token_y):
    return parity, (column_of(y, parity)[1] + token_y - y + N // 2) % N


WIDE = [
    [device(y, xh, *token_place(y, xh ^ rel, a), 0) for rel in (0, 1) for a in range(N)]
    for y in range(N)
    for xh in (0, 1)
] + [
    [device(a, xl ^ rel, xl, z, 1) for rel in (0, 1) for a in range(N)] for xl in (0, 1) for z in range(N)
]
ROW_GROUPS = [
    [device(a, xl ^ rel, xl, z, core) for rel in (0, 1) for a in range(N)]
    for core in (0, 1)
    for xl in (0, 1)
    for z in range(N)
]
NARROW = [[device(a, xh, xl, z, 0) for a in range(N)] for xh in (0, 1) for xl in (0, 1) for z in range(N)] + [
    [device(y, xh, xl, hidden_z(y, xh, a), 1) for a in range(N)] for y in range(N) for xh in (0, 1) for xl in (0, 1)
]

SWAP = [(d, d ^ 1) for d in range(4 * N * N * 2)]
PARTNER = [(device(y, xh, xl, z, 0), device(y, 1 - xh, xl, z, 0)) for y, xh, xl, z in CHIPS] + [
    (device(y, xh, xl, z, 1), device(y, xh, 1 - xl, z, 1)) for y, xh, xl, z in CHIPS
]
PARTNER_SWAP = [(device(y, xh, xl, z, 1), device(y, 1 - xh, xl, z, 0)) for y, xh, xl, z in CHIPS] + [
    (device(y, xh, xl, z, 0), device(y, xh, 1 - xl, z, 1)) for y, xh, xl, z in CHIPS
]
SWAP_PARTNER = [(there, here) for here, there in PARTNER_SWAP]


def spread(core):
    moves = []
    for y, xh, xl, z in CHIPS:
        column = xl * N + z
        row = column // 2
        moves.append((device(y, xh, xl, z, core), device(row, xh, *token_place(row, column % 2, y), 0)))
        moves.append((device(y, xh, xl, z, 1 - core), device(y, xl, xh, z, 1)))
    return moves


SPREAD = spread(0)
CROSS = [
    move
    for y, xh, xl, z in CHIPS
    for a in [(z - column_of(y, xh)[1] + y + N // 2) % N]
    for here, there in [(device(y, xh, xl, z, 1), device(a, xl, *column_of(y, xh), 0))]
    for move in ((here, there), (there, here))
]
BACK = [(device(y, xh, xl, z, core), device(y, xl, xh, z, core)) for y, xh, xl, z in CHIPS for core in (0, 1)]


def trade(blocks, groups):
    return lax.all_to_all(blocks, ALL, split_axis=0, concat_axis=0, axis_index_groups=groups, tiled=True)


def gather(block, groups):
    return trade(jnp.broadcast_to(block, (len(groups[0]),) + block.shape), groups)


def reduce(partial, groups):
    return jnp.sum(trade(partial.astype(jnp.bfloat16), groups).astype(jnp.float32), axis=0)


def unfold(tall):
    half = tall.shape[0] // 2
    return jnp.concatenate([tall[:half], tall[half:]], axis=1)


def wide_fold(wide):
    half = wide.shape[2] // 2
    return jnp.concatenate([wide[:, :, :half], wide[:, :, half:]], axis=1)


def wide_unfold(block):
    half = block.shape[0] // 2
    return jnp.concatenate([block[:half], block[half:]], axis=1)


def local(tokens, mixer_out, gate_weight, out_weight, out_grad):
    f32, bf16 = jnp.float32, jnp.bfloat16
    first = lax.axis_index("c") == 0
    inner, width = gate_weight.shape[1], out_grad.shape[1]
    half = gate_weight.shape[1] // 2
    to_first = jnp.concatenate([tokens, gate_weight[:, :half], gate_weight[:, half:]], axis=0)
    to_second = jnp.concatenate([out_grad, out_weight], axis=0)
    sent = with_layout_constraint(jnp.where(first, to_second, to_first), BY_ROWS)
    mine = jnp.where(first, tokens, out_grad)
    swapped = with_layout_constraint(lax.ppermute(sent, ALL, SWAP), BY_ROWS)
    pair = lax.ppermute(jnp.concatenate([mine, swapped[: mine.shape[0]]], axis=1), ALL, SPREAD)
    block = swapped[mine.shape[0] :]
    weight = jnp.where(
        first,
        jnp.concatenate([gate_weight, unfold(block)], axis=1),
        jnp.concatenate([out_weight, block], axis=1).T,
    )
    acts = gather(pair, WIDE)
    mixer_in = lax.ppermute(mixer_out, ALL, SWAP)
    acts, mixer_in = lax.optimization_barrier((acts, mixer_in))
    acts = acts.reshape(2, N * acts.shape[1], acts.shape[2])
    weight = jnp.stack([weight, lax.ppermute(weight, ALL, PARTNER)])
    mixer_vals = jnp.concatenate([mixer_out, mixer_in], axis=1).astype(f32)

    partial = jnp.einsum("kad,kdn->an", acts, weight, preferred_element_type=f32)
    total = reduce(partial.reshape(N, -1, partial.shape[1]), NARROW)

    gate_pre = total
    gate_sig = jax.nn.sigmoid(gate_pre)
    gate_silu = gate_pre * gate_sig
    gated = (mixer_vals * gate_silu).astype(bf16)
    crossed = lax.ppermute(jnp.where(first, gated, total.astype(bf16)), ALL, CROSS)
    hidden_grad = crossed.astype(f32)
    mixer_grad = (hidden_grad * gate_silu).astype(bf16)
    pre_grad = (hidden_grad * mixer_vals * gate_sig * (1.0 + gate_pre * (1.0 - gate_sig))).astype(bf16)
    units = gather(jnp.where(first, pre_grad, crossed), NARROW)
    mixer_grad_in = lax.ppermute(mixer_grad[:, inner:], ALL, SWAP)
    units, mixer_grad_in = lax.optimization_barrier((units, mixer_grad_in))
    units = units.reshape(-1, units.shape[2])

    def layer_part(start):
        return jnp.stack(
            [
                lax.dot_general(
                    units, w[start : start + width], (((1,), (1,)), ((), ())), preferred_element_type=f32
                ).astype(bf16)
                for w in weight
            ]
        )

    layer_in = lax.ppermute(layer_part(width), ALL, SWAP)
    layer_blocks = jnp.where(first, layer_in, layer_part(0))
    layer_own = reduce(layer_blocks.reshape(2 * N, -1, width), ROW_GROUPS).astype(bf16)

    grads = jnp.einsum("kad,an->kdn", acts, units, preferred_element_type=f32)
    keep = jnp.where(first, grads[:, :, :inner], wide_fold(grads[:, :width]))
    send = jnp.where(first, grads[:, :, inner:], wide_fold(grads[:, width:]))
    swap_in = lax.ppermute(send[0], ALL, SWAP)
    keep_far, send_far = keep[1].astype(bf16), send[1].astype(bf16)
    layer_out = lax.ppermute(layer_own, ALL, BACK)
    kept = (keep[0] + lax.ppermute(keep_far, ALL, PARTNER).astype(f32)).astype(bf16)
    sent = (swap_in + lax.ppermute(send_far, ALL, SWAP_PARTNER).astype(f32)).astype(bf16)
    return (
        layer_out,
        jnp.where(first, mixer_grad[:, :inner], mixer_grad_in),
        jnp.where(first, kept, sent),
        wide_unfold(jnp.where(first, sent, kept)).T,
    )


def solution(mesh):
    fine = Mesh(mesh.devices.reshape(N, 2, 2, N, 2), ALL)
    spec = P(ROWS, COLS)
    return jax.shard_map(local, mesh=fine, in_specs=(spec,) * 5, out_specs=(spec,) * 4, check_vma=False)
```

```python
import jax
import jax.numpy as jnp
from jax import lax
from jax.experimental.layout import Layout, with_layout_constraint
from jax.sharding import Mesh, PartitionSpec as P

ROWS, COLS = ("y", "xh"), ("xl", "z", "c")
ALL = ROWS + COLS
BY_ROWS = Layout(major_to_minor=(0, 1))
N = 8


def device(y, xh, xl, z, core):
    return (((y * 2 + xh) * 2 + xl) * N + z) * 2 + core


CHIPS = [(y, xh, xl, z) for y in range(N) for xh in (0, 1) for xl in (0, 1) for z in range(N)]


def column_of(y, xh):
    return y // 4, (y % 4) * 2 + xh


def hidden_z(y, xh, token_y):
    return (column_of(y, xh)[1] + token_y - y + N // 2) % N


def token_place(y, parity, token_y):
    return parity, (column_of(y, parity)[1] + token_y - y + N // 2) % N


WIDE = [
    [device(y, xh, *token_place(y, xh ^ rel, a), 0) for rel in (0, 1) for a in range(N)]
    for y in range(N)
    for xh in (0, 1)
] + [
    [device(a, xl ^ rel, xl, z, 1) for rel in (0, 1) for a in range(N)] for xl in (0, 1) for z in range(N)
]
ROW_GROUPS = [
    [device(a, xl ^ rel, xl, z, core) for rel in (0, 1) for a in range(N)]
    for core in (0, 1)
    for xl in (0, 1)
    for z in range(N)
]
NARROW = [[device(a, xh, xl, z, 0) for a in range(N)] for xh in (0, 1) for xl in (0, 1) for z in range(N)] + [
    [device(y, xh, xl, hidden_z(y, xh, a), 1) for a in range(N)] for y in range(N) for xh in (0, 1) for xl in (0, 1)
]

SWAP = [(d, d ^ 1) for d in range(4 * N * N * 2)]
PARTNER = [(device(y, xh, xl, z, 0), device(y, 1 - xh, xl, z, 0)) for y, xh, xl, z in CHIPS] + [
    (device(y, xh, xl, z, 1), device(y, xh, 1 - xl, z, 1)) for y, xh, xl, z in CHIPS
]
PARTNER_SWAP = [(device(y, xh, xl, z, 1), device(y, 1 - xh, xl, z, 0)) for y, xh, xl, z in CHIPS] + [
    (device(y, xh, xl, z, 0), device(y, xh, 1 - xl, z, 1)) for y, xh, xl, z in CHIPS
]
SWAP_PARTNER = [(there, here) for here, there in PARTNER_SWAP]


def spread(core):
    moves = []
    for y, xh, xl, z in CHIPS:
        column = xl * N + z
        row = column // 2
        moves.append((device(y, xh, xl, z, core), device(row, xh, *token_place(row, column % 2, y), 0)))
        moves.append((device(y, xh, xl, z, 1 - core), device(y, xl, xh, z, 1)))
    return moves


SPREAD = spread(0)
CROSS = [
    move
    for y, xh, xl, z in CHIPS
    for a in [(z - column_of(y, xh)[1] + y + N // 2) % N]
    for here, there in [(device(y, xh, xl, z, 1), device(a, xl, *column_of(y, xh), 0))]
    for move in ((here, there), (there, here))
]
BACK = [(device(y, xh, xl, z, core), device(y, xl, xh, z, core)) for y, xh, xl, z in CHIPS for core in (0, 1)]


def trade(blocks, groups):
    return lax.all_to_all(blocks, ALL, split_axis=0, concat_axis=0, axis_index_groups=groups, tiled=True)


def gather(block, groups):
    return trade(jnp.broadcast_to(block, (len(groups[0]),) + block.shape), groups)


def reduce(partial, groups):
    return jnp.sum(trade(partial.astype(jnp.bfloat16), groups).astype(jnp.float32), axis=0)


def unfold(tall):
    half = tall.shape[0] // 2
    return jnp.concatenate([tall[:half], tall[half:]], axis=1)


def wide_fold(wide):
    half = wide.shape[2] // 2
    return jnp.concatenate([wide[:, :, :half], wide[:, :, half:]], axis=1)


def wide_unfold(block):
    half = block.shape[0] // 2
    return jnp.concatenate([block[:half], block[half:]], axis=1)


def local(tokens, mixer_out, gate_weight, out_weight, out_grad):
    f32, bf16 = jnp.float32, jnp.bfloat16
    first = lax.axis_index("c") == 0
    inner, width = gate_weight.shape[1], out_grad.shape[1]
    half = gate_weight.shape[1] // 2
    to_first = jnp.concatenate([tokens, gate_weight[:, :half], gate_weight[:, half:]], axis=0)
    to_second = jnp.concatenate([out_grad, out_weight], axis=0)
    sent = with_layout_constraint(jnp.where(first, to_second, to_first), BY_ROWS)
    mine = jnp.where(first, tokens, out_grad)
    swapped = with_layout_constraint(lax.ppermute(sent, ALL, SWAP), BY_ROWS)
    pair = lax.ppermute(jnp.concatenate([mine, swapped[: mine.shape[0]]], axis=1), ALL, SPREAD)
    block = swapped[mine.shape[0] :]
    weight = jnp.where(
        first,
        jnp.concatenate([gate_weight, unfold(block)], axis=1),
        jnp.concatenate([out_weight, block], axis=1).T,
    )
    acts = gather(pair, WIDE)
    mixer_in = lax.ppermute(mixer_out, ALL, SWAP)
    acts, mixer_in = lax.optimization_barrier((acts, mixer_in))
    acts = acts.reshape(2, N * acts.shape[1], acts.shape[2])
    weight = jnp.stack([weight, lax.ppermute(weight, ALL, PARTNER)])
    mixer_vals = jnp.concatenate([mixer_out, mixer_in], axis=1).astype(f32)

    partial = jnp.einsum("kad,kdn->an", acts, weight, preferred_element_type=f32)
    total = reduce(partial.reshape(N, -1, partial.shape[1]), NARROW)

    gate_pre = total
    gate_sig = jax.nn.sigmoid(gate_pre)
    gate_silu = gate_pre * gate_sig
    gated = (mixer_vals * gate_silu).astype(bf16)
    crossed = lax.ppermute(jnp.where(first, gated, total.astype(bf16)), ALL, CROSS)
    hidden_grad = crossed.astype(f32)
    mixer_grad = (hidden_grad * gate_silu).astype(bf16)
    pre_grad = (hidden_grad * mixer_vals * gate_sig * (1.0 + gate_pre * (1.0 - gate_sig))).astype(bf16)
    units = gather(jnp.where(first, pre_grad, crossed), NARROW)
    mixer_grad_in = lax.ppermute(mixer_grad[:, inner:], ALL, SWAP)
    units, mixer_grad_in = lax.optimization_barrier((units, mixer_grad_in))
    units = units.reshape(-1, units.shape[2])

    def layer_part(units, start):
        return jnp.stack(
            [
                lax.dot_general(
                    units, w[start : start + width], (((1,), (1,)), ((), ())), preferred_element_type=f32
                ).astype(bf16)
                for w in weight
            ]
        )

    layer_sent, units = lax.optimization_barrier((layer_part(units, width), units))
    layer_in = lax.ppermute(layer_sent, ALL, SWAP)
    layer_blocks = jnp.where(first, layer_in, layer_part(units, 0))
    layer_own = reduce(layer_blocks.reshape(2 * N, -1, width), ROW_GROUPS).astype(bf16)

    grads = jnp.einsum("kad,an->kdn", acts, units, preferred_element_type=f32)
    keep = jnp.where(first, grads[:, :, :inner], wide_fold(grads[:, :width]))
    send = jnp.where(first, grads[:, :, inner:], wide_fold(grads[:, width:]))
    swap_in = lax.ppermute(send[0], ALL, SWAP)
    keep_far, send_far = keep[1].astype(bf16), send[1].astype(bf16)
    layer_out = lax.ppermute(layer_own, ALL, BACK)
    kept = (keep[0] + lax.ppermute(keep_far, ALL, PARTNER).astype(f32)).astype(bf16)
    sent = (swap_in + lax.ppermute(send_far, ALL, SWAP_PARTNER).astype(f32)).astype(bf16)
    return (
        layer_out,
        jnp.where(first, mixer_grad[:, :inner], mixer_grad_in),
        jnp.where(first, kept, sent),
        wide_unfold(jnp.where(first, sent, kept)).T,
    )


def solution(mesh):
    fine = Mesh(mesh.devices.reshape(N, 2, 2, N, 2), ALL)
    spec = P(ROWS, COLS)
    return jax.shard_map(local, mesh=fine, in_specs=(spec,) * 5, out_specs=(spec,) * 4, check_vma=False)
```
